32 devices in a mesh: gx: 8 (over z, y), gy: 4 (over x, core).
Axes of the slice: x: 2, y: 2, z: 4, core: 2. Of those that a mesh axis runs over, the one named last changes fastest.
Arguments:
- state_field: float32 [256, 256, 1, 8, 256], P('gx', 'gy'), may hold values from -42 to 42
- start_one: float32 [256, 128], replicated, may hold values from -0.375 to 0.375
- start_two: float32 [256, 128], replicated, may hold values from -0.375 to 0.375
Outputs:
- core_tensor: float32 [128, 128, 1, 8, 256], P('gy', None, None, None, 'gx')
- factor_one: float32 [256, 128], replicated
- factor_two: float32 [256, 128], replicated
The draws below stay inside these ranges and needn't reach their ends.
All inputs are finite; a program needn't handle non-finite values.
Results may differ from the reference program's by a relative error of at most 0.00024.
Values sent between devices are 32-bit elements; how exact they have to be, the bound alone decides.
A program may use at most 256 MiB of HBM per device.

```python
import math
import jax
import jax.numpy as jnp
from jax import lax

N1 = 256
N2 = 256
N3 = 256
V = 8
SNAP = 1
RANK = 128
SWEEPS = 2


def draw_state_field(key, part):
    key = jax.random.fold_in(key, 11)
    subkeys = jax.random.split(key, 6)
    full_shape = (N1, N2, SNAP, V, N3)
    row_scale = jnp.exp(jax.random.uniform(subkeys[0], (N1,), jnp.float32, 0.0, math.log(2.5)))
    column_scale = jnp.exp(jax.random.uniform(subkeys[1], (N2,), jnp.float32, 0.0, math.log(2.5)))
    fluctuation = jnp.clip(jax.random.normal(subkeys[2], full_shape, jnp.float32), -5.0, 5.0)
    amplitude = 0.15
    mode_one = jax.random.uniform(subkeys[3], (3, N1), jnp.float32, -1.5, 1.5)
    mode_two = jax.random.uniform(subkeys[4], (3, N2), jnp.float32, -1.5, 1.5)
    profile = jax.random.uniform(subkeys[5], (3, SNAP, V, N3), jnp.float32, -1.5, 1.5)
    structured = fluctuation
    for component in range(3):
        structured = structured + amplitude * (mode_one[component][:, None, None, None, None] * mode_two[component][None, :, None, None, None] * profile[component][None, None])
    return row_scale[:, None, None, None, None] * column_scale[None, :, None, None, None] * structured


def noise(stream_key, shape, scale, most, dtype=jnp.bfloat16):
    return jnp.clip(scale * jax.random.normal(stream_key, shape, jnp.float32), -most, most).astype(dtype)


def setup_inputs(seed: int = 0) -> dict:
    streams_of = jax.random.split(jax.random.key(seed), 4)
    return {
        "state_field": draw_state_field(jax.random.fold_in(streams_of[3], 71), 0),
        "start_one": noise(streams_of[1], (N1, RANK), N1 ** -0.5, 0.375, jnp.float32),
        "start_two": noise(streams_of[2], (N2, RANK), N2 ** -0.5, 0.375, jnp.float32),
    }


def orthonormalize(projected):
    products = jnp.dot(projected.T.astype(jnp.float32), projected.astype(jnp.float32), precision=lax.Precision.HIGHEST, preferred_element_type=jnp.float32)
    lower_factor = jnp.linalg.cholesky(products)
    return jax.scipy.linalg.solve_triangular(lower_factor, projected.T, lower=True).T

def subspace(gram_matrix, basis):
    for iteration in range(SWEEPS):
        projected = jnp.dot(gram_matrix.astype(jnp.float32), basis.astype(jnp.float32), precision=lax.Precision.HIGHEST, preferred_element_type=jnp.float32)
        basis = orthonormalize(projected)
    return basis

def reference(state_field, start_one, start_two):
    unfolded = state_field.reshape(N1, -1)
    gram_one = jnp.dot(unfolded.astype(jnp.float32), unfolded.T.astype(jnp.float32), precision=lax.Precision.HIGHEST, preferred_element_type=jnp.float32)
    factor_one = subspace(gram_one, start_one)
    reduced = jnp.dot(factor_one.T.astype(jnp.float32), unfolded.astype(jnp.float32), precision=lax.Precision.HIGHEST, preferred_element_type=jnp.float32)
    reduced = reduced.reshape(RANK, N2, -1)
    gram_two = jnp.einsum('rjx,rkx->jk', reduced, reduced, precision=lax.Precision.HIGHEST)
    factor_two = subspace(gram_two, start_two)
    core_tensor = jnp.einsum('js,rjx->rsx', factor_two, reduced, precision=lax.Precision.HIGHEST)
    return (core_tensor.reshape(RANK, RANK, SNAP, V, N3), factor_one, factor_two)
```

```python
import functools

import jax
import jax.numpy as jnp
from jax import lax
from jax.experimental import pallas as pl
from jax.experimental.pallas import tpu as pltpu
from jax.sharding import PartitionSpec as P

SWEEPS = 2
LANES = 128
MESH = pl.DeviceIdType.MESH
F32 = jnp.float32
BF16 = jnp.bfloat16
NT = (((1,), (1,)), ((), ()))
TN = (((0,), (0,)), ((), ()))
NN = (((1,), (0,)), ((), ()))
VMEM_LIMIT = 48 * 1024 * 1024


def split(x):
    high = x.astype(BF16)
    return high, (x - high.astype(F32)).astype(BF16)


def product(a, b, dims):
    (ah, al), (bh, bl) = a, b
    dot = functools.partial(lax.dot_general, dimension_numbers=dims, preferred_element_type=F32)
    return dot(ah, bh) + (dot(ah, bl) + dot(al, bh))


def relayout_kernel(width, variables, x_ref, o_ref):
    per = LANES // width
    rows = x_ref.shape[0] // 8
    groups = variables // per
    lane = lax.broadcasted_iota(jnp.int32, (8, LANES), 1)

    def body(j, carry):
        for h in range(groups):
            regs = [
                x_ref[pl.ds(j * variables + h * per + k, 8, stride=rows), :] for k in range(per)
            ]
            step = per // 2
            while step:
                first = (lane // (width * step)) % 2 == 0
                for k in range(per):
                    if (k // step) % 2 == 0:
                        a, b = regs[k], regs[k + step]
                        regs[k] = jnp.where(first, a, pltpu.roll(b, width * step, 1))
                        regs[k + step] = jnp.where(
                            first, pltpu.roll(a, LANES - width * step, 1), b
                        )
                step //= 2
            for g in range(per):
                o_ref[g, j, :, h * LANES : (h + 1) * LANES] = regs[g]
        return carry

    lax.fori_loop(0, rows // variables, body, 0, unroll=2)


def relayout(field, parts):
    rows_one, rows_two, snapshots, variables, cells = field.shape
    inner = snapshots * variables
    width = cells // parts
    per = LANES // width
    halves = cells // LANES
    flat = field.reshape(rows_one * rows_two * inner, cells)
    return pl.pallas_call(
        functools.partial(relayout_kernel, width, inner),
        grid=(rows_one // 8, halves),
        in_specs=[pl.BlockSpec((8 * rows_two * inner, LANES), lambda i, h: (i, h))],
        out_specs=pl.BlockSpec((per, rows_two, 8, inner * width), lambda i, h: (h, 0, i, 0)),
        out_shape=jax.ShapeDtypeStruct((parts, rows_two, rows_one, inner * width), F32),
        compiler_params=pltpu.CompilerParams(vmem_limit_bytes=VMEM_LIMIT),
    )(flat)


def greet(axis, size):
    me = lax.axis_index(axis)
    barrier = pltpu.get_barrier_semaphore()
    for off in range(1, size):
        pl.semaphore_signal(
            barrier, inc=1, device_id={axis: lax.rem(me + off, size)}, device_id_type=MESH
        )


def gather_kernel(n, chunks, l_ref, u_ref, g_ref, buf, hh, hl, send, recv, own, load):
    me = lax.axis_index("gx")
    depth = l_ref.shape[1] // chunks
    rows = l_ref.shape[2]
    greet("gx", n)
    pl.semaphore_wait(pltpu.get_barrier_semaphore(), n - 1)

    def copy(c, off):
        peer = lax.rem(me + off, n)
        return pltpu.make_async_remote_copy(
            src_ref=l_ref.at[peer, pl.ds(c * depth, depth)],
            dst_ref=u_ref.at[pl.ds(c * depth, depth), pl.ds(me * rows, rows)],
            send_sem=send.at[c, off - 1],
            recv_sem=recv.at[c, off - 1],
            device_id={"gx": peer},
            device_id_type=MESH,
        )

    def keep(c):
        return pltpu.make_async_copy(
            l_ref.at[me, pl.ds(c * depth, depth)],
            u_ref.at[pl.ds(c * depth, depth), pl.ds(me * rows, rows)],
            own.at[c],
        )

    def start(c, carry):
        for off in range(1, n):
            copy(c, off).start()
        keep(c).start()
        return carry

    lax.fori_loop(0, chunks, start, 0)
    hh[...] = jnp.zeros_like(hh)
    hl[...] = jnp.zeros_like(hl)

    def work(c, carry):
        for off in range(1, n):
            copy(c, off).wait_recv()
        keep(c).wait()
        fetch = pltpu.make_async_copy(u_ref.at[pl.ds(c * depth, depth)], buf, load)
        fetch.start()
        fetch.wait()

        def one(j, carry):
            high, low = split(buf[j])
            hh[...] += lax.dot_general(high, high, NT, preferred_element_type=F32)
            hl[...] += lax.dot_general(high, low, NT, preferred_element_type=F32)
            return carry

        lax.fori_loop(0, depth, one, 0, unroll=2)
        return carry

    lax.fori_loop(0, chunks, work, 0)
    cross = hl[...]
    g_ref[...] = hh[...] + (cross + cross.T)

    def finish(c, carry):
        for off in range(1, n):
            copy(c, off).wait_send()
        return carry

    lax.fori_loop(0, chunks, finish, 0)


def gather(blocks, chunks):
    n, rows_two, rows_one, width = blocks.shape
    total = n * rows_one
    return pl.pallas_call(
        functools.partial(gather_kernel, n, chunks),
        in_specs=[pl.BlockSpec(memory_space=pl.ANY)],
        out_specs=[pl.BlockSpec(memory_space=pl.ANY), pl.BlockSpec(memory_space=pltpu.VMEM)],
        out_shape=[
            jax.ShapeDtypeStruct((rows_two, total, width), F32),
            jax.ShapeDtypeStruct((total, total), F32),
        ],
        scratch_shapes=[
            pltpu.VMEM((rows_two // chunks, total, width), F32),
            pltpu.VMEM((total, total), F32),
            pltpu.VMEM((total, total), F32),
            pltpu.SemaphoreType.DMA((chunks, n - 1)),
            pltpu.SemaphoreType.DMA((chunks, n - 1)),
            pltpu.SemaphoreType.DMA((chunks,)),
            pltpu.SemaphoreType.DMA,
        ],
        compiler_params=pltpu.CompilerParams(
            collective_id=0, has_side_effects=True, vmem_limit_bytes=VMEM_LIMIT
        ),
    )(blocks)


def sum_kernel(nx, ny, p_ref, o_ref, got_y, part, got_x, s1, r1, s2, r2, s3, r3, s4, r4):
    mx, my = lax.axis_index("gx"), lax.axis_index("gy")
    greet("gx", nx)
    greet("gy", ny)
    pl.semaphore_wait(pltpu.get_barrier_semaphore(), nx + ny - 2)

    def push(axis, me, size, source, target, send, recv):
        copies = []
        for off in range(1, size):
            peer = lax.rem(me + off, size)
            copies.append(
                pltpu.make_async_remote_copy(
                    src_ref=source(peer),
                    dst_ref=target(off),
                    send_sem=send.at[off - 1],
                    recv_sem=recv.at[off - 1],
                    device_id={axis: peer},
                    device_id_type=MESH,
                )
            )
        for c in copies:
            c.start()
        return copies

    first = push("gy", my, ny, lambda p: p_ref.at[p], lambda off: got_y.at[off - 1], s1, r1)
    for c in first:
        c.wait_recv()
    total = p_ref[my]
    for off in range(1, ny):
        total = total + got_y[off - 1]
    part[...] = total
    second = push("gx", mx, nx, lambda p: part.at[p], lambda off: got_x.at[off - 1], s2, r2)
    for c in second:
        c.wait_recv()
    total = part[mx]
    for off in range(1, nx):
        total = total + got_x[off - 1]
    o_ref[my, mx] = total
    third = push("gx", mx, nx, lambda p: o_ref.at[my, mx], lambda off: o_ref.at[my, mx], s3, r3)
    for c in third:
        c.wait_recv()
    fourth = push("gy", my, ny, lambda p: o_ref.at[my], lambda off: o_ref.at[my], s4, r4)
    for c in fourth:
        c.wait_recv()
    for c in first + second + third + fourth:
        c.wait_send()


def sum_all(matrix, nx, ny, collective):
    rows, columns = matrix.shape
    small = rows // (nx * ny)
    blocks = matrix.reshape(ny, nx, small, columns)
    out = pl.pallas_call(
        functools.partial(sum_kernel, nx, ny),
        in_specs=[pl.BlockSpec(memory_space=pltpu.VMEM)],
        out_specs=pl.BlockSpec(memory_space=pltpu.VMEM),
        out_shape=jax.ShapeDtypeStruct(blocks.shape, F32),
        scratch_shapes=[
            pltpu.VMEM((ny - 1, nx, small, columns), F32),
            pltpu.VMEM((nx, small, columns), F32),
            pltpu.VMEM((nx - 1, small, columns), F32),
        ]
        + [pltpu.SemaphoreType.DMA((k - 1,)) for k in (ny, ny, nx, nx, nx, nx, ny, ny)],
        compiler_params=pltpu.CompilerParams(
            collective_id=collective, has_side_effects=True, vmem_limit_bytes=VMEM_LIMIT
        ),
    )(blocks)
    return out.reshape(rows, columns)


def reduce_kernel(n, chunks, u_ref, f_ref, r_ref, buf, out, send, recv, own, load):
    me = lax.axis_index("gy")
    columns = u_ref.shape[0]
    depth = columns // chunks
    ranks = r_ref.shape[1]
    greet("gy", n)
    pl.semaphore_wait(pltpu.get_barrier_semaphore(), n - 1)
    factor = split(f_ref[...].T)

    def fetch(c):
        slot = lax.rem(c, 2)
        return pltpu.make_async_copy(
            u_ref.at[pl.ds(c * depth, depth)], buf.at[slot], load.at[slot]
        )

    def copy(c, off):
        peer = lax.rem(me + off, n)
        return pltpu.make_async_remote_copy(
            src_ref=out.at[pl.ds(c * depth, depth), pl.ds(peer * ranks, ranks)],
            dst_ref=r_ref.at[pl.ds(me * columns + c * depth, depth)],
            send_sem=send.at[c, off - 1],
            recv_sem=recv.at[c, off - 1],
            device_id={"gy": peer},
            device_id_type=MESH,
        )

    def keep(c):
        return pltpu.make_async_copy(
            out.at[pl.ds(c * depth, depth), pl.ds(me * ranks, ranks)],
            r_ref.at[pl.ds(me * columns + c * depth, depth)],
            own.at[c],
        )

    fetch(0).start()

    def work(c, carry):
        @pl.when(c + 1 < chunks)
        def _():
            fetch(c + 1).start()

        fetch(c).wait()
        slot = lax.rem(c, 2)

        def one(j, carry):
            out[c * depth + j] = product(factor, split(buf[slot, j]), NN)
            return carry

        lax.fori_loop(0, depth, one, 0, unroll=2)
        for off in range(1, n):
            copy(c, off).start()
        keep(c).start()
        return carry

    lax.fori_loop(0, chunks, work, 0)

    def finish(c, carry):
        for off in range(1, n):
            copy(c, off).wait_recv()
            copy(c, off).wait_send()
        keep(c).wait()
        return carry

    lax.fori_loop(0, chunks, finish, 0)


def reduce_exchange(unfolded, factor, n, chunks):
    columns, rows, width = unfolded.shape
    rank = factor.shape[1]
    return pl.pallas_call(
        functools.partial(reduce_kernel, n, chunks),
        in_specs=[pl.BlockSpec(memory_space=pl.ANY), pl.BlockSpec(memory_space=pltpu.VMEM)],
        out_specs=pl.BlockSpec(memory_space=pl.ANY),
        out_shape=jax.ShapeDtypeStruct((n * columns, rank // n, width), F32),
        scratch_shapes=[
            pltpu.VMEM((2, columns // chunks, rows, width), F32),
            pltpu.VMEM((columns, rank, width), F32),
            pltpu.SemaphoreType.DMA((chunks, n - 1)),
            pltpu.SemaphoreType.DMA((chunks, n - 1)),
            pltpu.SemaphoreType.DMA((chunks,)),
            pltpu.SemaphoreType.DMA((2,)),
        ],
        compiler_params=pltpu.CompilerParams(
            collective_id=2, has_side_effects=True, vmem_limit_bytes=VMEM_LIMIT
        ),
    )(unfolded, factor)


def rank_slice(refs, r):
    rows = refs[0].shape[0]
    parts = [
        ref.reshape(rows * 8, LANES)[pl.ds(r, rows, stride=8), :] for ref in refs
    ]
    return parts[0] if len(parts) == 1 else jnp.concatenate(parts, axis=1)


def gram_kernel(halves, *refs):
    *x_refs, g_ref, hh, hl = refs
    step = pl.program_id(0)

    @pl.when(step == 0)
    def _():
        hh[...] = jnp.zeros_like(hh)
        hl[...] = jnp.zeros_like(hl)

    for r in range(8):
        high, low = split(rank_slice(x_refs, r))
        hh[...] += lax.dot_general(high, high, NT, preferred_element_type=F32)
        hl[...] += lax.dot_general(high, low, NT, preferred_element_type=F32)

    @pl.when(step == pl.num_programs(0) - 1)
    def _():
        cross = hl[...]
        g_ref[...] = hh[...] + (cross + cross.T)


def half_specs(rows, halves):
    return [
        pl.BlockSpec((rows, 8, LANES), functools.partial(lambda h, r: (0, r, h), h))
        for h in range(halves)
    ]


def gram(reduced):
    rows, ranks, width = reduced.shape
    halves = width // LANES
    return pl.pallas_call(
        functools.partial(gram_kernel, halves),
        grid=(ranks // 8,),
        in_specs=half_specs(rows, halves),
        out_specs=pl.BlockSpec((rows, rows), lambda r: (0, 0)),
        out_shape=jax.ShapeDtypeStruct((rows, rows), F32),
        scratch_shapes=[pltpu.VMEM((rows, rows), F32), pltpu.VMEM((rows, rows), F32)],
        compiler_params=pltpu.CompilerParams(vmem_limit_bytes=VMEM_LIMIT),
    )(*[reduced] * halves)


def core_kernel(halves, *refs):
    *x_refs, f_ref, o_ref = refs
    factor = split(f_ref[...])
    for r in range(8):
        o_ref[r] = product(split(rank_slice(x_refs, r).T), factor, NN)


def core(reduced, factor):
    rows, ranks, width = reduced.shape
    halves = width // LANES
    kept = factor.shape[1]
    return pl.pallas_call(
        functools.partial(core_kernel, halves),
        grid=(ranks // 8,),
        in_specs=half_specs(rows, halves) + [pl.BlockSpec((rows, kept), lambda r: (0, 0))],
        out_specs=pl.BlockSpec((8, width, kept), lambda r: (r, 0, 0)),
        out_shape=jax.ShapeDtypeStruct((ranks, width, kept), F32),
        compiler_params=pltpu.CompilerParams(vmem_limit_bytes=VMEM_LIMIT),
    )(*[reduced] * halves, factor)


def orthonormalize_rows(projected, products):
    lower_factor = jnp.linalg.cholesky(products)
    return jax.scipy.linalg.solve_triangular(lower_factor, projected.T, lower=True).T


def subspace(gram_matrix, basis):
    dot = functools.partial(
        jnp.dot, precision=lax.Precision.HIGHEST, preferred_element_type=F32
    )
    for iteration in range(SWEEPS):
        projected = dot(gram_matrix, basis)
        basis = orthonormalize_rows(projected, dot(projected.T, projected))
    return basis


def shards(nx, ny, state_field, start_one, start_two):
    snapshots, variables, cells = state_field.shape[2:]
    rank = start_one.shape[1]
    chunks = 8
    blocks = relayout(state_field, nx)
    unfolded, partial_one = gather(blocks, chunks)
    factor_one = subspace(sum_all(partial_one, nx, ny, 1), start_one)
    reduced = reduce_exchange(unfolded, factor_one, ny, chunks)
    factor_two = subspace(sum_all(gram(reduced), nx, ny, 1), start_two)
    packed = core(reduced, factor_two)
    packed = packed.reshape(rank // ny, snapshots, variables, cells // nx, rank)
    return packed.transpose(0, 4, 1, 2, 3), factor_one, factor_two


def solution(mesh):
    placed = (P("gx", "gy", None, None, None), P(), P())
    return jax.shard_map(
        functools.partial(shards, mesh.shape["gx"], mesh.shape["gy"]),
        mesh=mesh,
        in_specs=placed,
        out_specs=(P("gy", None, None, None, "gx"), P(), P()),
        check_vma=False,
    )
```

```python
import functools

import jax
import jax.numpy as jnp
from jax import lax
from jax.experimental import pallas as pl
from jax.experimental.pallas import tpu as pltpu
from jax.sharding import PartitionSpec as P

SWEEPS = 2
LANES = 128
MESH = pl.DeviceIdType.MESH
F32 = jnp.float32
BF16 = jnp.bfloat16
NT = (((1,), (1,)), ((), ()))
TN = (((0,), (0,)), ((), ()))
NN = (((1,), (0,)), ((), ()))
VMEM_LIMIT = 48 * 1024 * 1024


def split(x):
    high = x.astype(BF16)
    return high, (x - high.astype(F32)).astype(BF16)


def product(a, b, dims):
    (ah, al), (bh, bl) = a, b
    dot = functools.partial(lax.dot_general, dimension_numbers=dims, preferred_element_type=F32)
    return dot(ah, bh) + (dot(ah, bl) + dot(al, bh))


def relayout(width, variables, x_ref, o_ref):
    halves, rows, held, _ = x_ref.shape
    per = LANES // width
    lane = lax.broadcasted_iota(jnp.int32, (8, LANES), 1)

    def body(t, carry):
        j, octet = t // (rows // 8), lax.rem(t, rows // 8)
        for half in range(halves):
            flat = x_ref.at[half].reshape(rows * held, LANES)
            for h in range(variables // per):
                base = octet * 8 * held + j * variables + h * per
                regs = [flat[pl.ds(base + k, 8, stride=held), :] for k in range(per)]
                step = per // 2
                while step:
                    first = (lane // (width * step)) % 2 == 0
                    for k in range(per):
                        if (k // step) % 2 == 0:
                            a, b = regs[k], regs[k + step]
                            regs[k] = jnp.where(first, a, pltpu.roll(b, width * step, 1))
                            regs[k + step] = jnp.where(
                                first, pltpu.roll(a, LANES - width * step, 1), b
                            )
                    step //= 2
                for g in range(per):
                    o_ref[
                        half * per + g,
                        j,
                        pl.ds(pl.multiple_of(octet * 8, 8), 8),
                        h * LANES : (h + 1) * LANES,
                    ] = regs[g]
        return carry

    lax.fori_loop(0, held // variables * (rows // 8), body, 0)


def greet(axis, size):
    me = lax.axis_index(axis)
    barrier = pltpu.get_barrier_semaphore()
    for off in range(1, size):
        pl.semaphore_signal(
            barrier, inc=1, device_id={axis: lax.rem(me + off, size)}, device_id_type=MESH
        )


def gather_kernel(
    n, ny, chunks, passed, variables, x_ref, v_ref, g_ref,
    xb, ob, buf, hh, hl, send, recv, own, load, fill, xs, xr, bs, br, cs, cr,
):
    me, my = lax.axis_index("gx"), lax.axis_index("gy")
    nc = ny // 2
    place, side = my // 2, lax.rem(my, 2)
    sibling = place * 2 + 1 - side
    depth, rows, width = ob.shape[2:]
    held = depth * variables
    lag = 2

    greet("gx", n)
    barrier = pltpu.get_barrier_semaphore()
    for off in range(1, nc):
        pl.semaphore_signal(
            barrier,
            inc=1,
            device_id={"gy": lax.rem(place + off, nc) * 2 + side},
            device_id_type=MESH,
        )
    pl.semaphore_signal(barrier, inc=1, device_id={"gy": sibling}, device_id_type=MESH)
    pl.semaphore_wait(barrier, n - 1 + nc)

    def take(c, half):
        slot = lax.rem(c, 2)
        return pltpu.make_async_copy(
            x_ref.at[:, pl.ds(c * held, held), pl.ds(half * LANES, LANES)],
            xb.at[slot, half],
            load.at[slot, half],
        )

    def span(c):
        return pl.ds(c * depth, depth)

    def copy(c, off):
        peer = lax.rem(me + off, n)
        return pltpu.make_async_remote_copy(
            src_ref=ob.at[c, peer],
            dst_ref=v_ref.at[my, span(c), pl.ds(me * rows, rows)],
            send_sem=send.at[c, off - 1],
            recv_sem=recv.at[c, off - 1],
            device_id={"gx": peer},
            device_id_type=MESH,
        )

    def keep(c):
        return pltpu.make_async_copy(
            ob.at[c, me], v_ref.at[my, span(c), pl.ds(me * rows, rows)], own.at[c]
        )

    def along(c, off):
        return pltpu.make_async_remote_copy(
            src_ref=v_ref.at[my, span(c)],
            dst_ref=v_ref.at[my, span(c)],
            send_sem=xs.at[c, off - 1],
            recv_sem=xr.at[c, off - 1],
            device_id={"gy": lax.rem(place + off, nc) * 2 + side},
            device_id_type=MESH,
        )

    def across(c):
        return pltpu.make_async_remote_copy(
            src_ref=v_ref.at[my, span(c)],
            dst_ref=v_ref.at[my, span(c)],
            send_sem=bs.at[c],
            recv_sem=br.at[c],
            device_id={"gy": sibling},
            device_id_type=MESH,
        )

    def onward(c, off):
        origin = lax.rem(place + nc - off, nc) * 2 + side
        return pltpu.make_async_remote_copy(
            src_ref=v_ref.at[origin, span(c)],
            dst_ref=v_ref.at[origin, span(c)],
            send_sem=cs.at[c, off - 1],
            recv_sem=cr.at[c, off - 1],
            device_id={"gy": sibling},
            device_id_type=MESH,
        )

    halves = xb.shape[1]
    for half in range(halves):
        take(0, half).start()

    def start(c, carry):
        @pl.when(c + 1 < chunks)
        def _():
            for half in range(halves):
                take(c + 1, half).start()

        for half in range(halves):
            take(c, half).wait()
        relayout(width // variables, variables, xb.at[lax.rem(c, 2)], ob.at[c])
        for off in range(1, n):
            copy(c, off).start()
        keep(c).start()
        return carry

    lax.fori_loop(0, chunks, start, 0)
    hh[...] = jnp.zeros_like(hh)
    hl[...] = jnp.zeros_like(hl)

    def work(c, carry):
        for off in range(1, n):
            copy(c, off).wait_recv()
        keep(c).wait()
        fetch = pltpu.make_async_copy(v_ref.at[my, span(c)], buf, fill)
        fetch.start()

        @pl.when(c < passed)
        def _():
            for off in range(1, nc):
                along(c, off).start()
            across(c).start()

        late = c - lag

        @pl.when((late >= 0) & (late < passed))
        def _():
            for off in range(1, nc):
                along(late, off).wait_recv()
                onward(late, off).start()

        fetch.wait()

        def one(j, carry):
            high, low = split(buf[j])
            hh[...] += lax.dot_general(high, high, NT, preferred_element_type=F32)
            hl[...] += lax.dot_general(high, low, NT, preferred_element_type=F32)
            return carry

        lax.fori_loop(0, depth, one, 0)
        return carry

    lax.fori_loop(0, chunks, work, 0)
    cross = hl[...]
    g_ref[...] = hh[...] + (cross + cross.T)

    def finish(c, carry):
        for off in range(1, n):
            copy(c, off).wait_send()

        @pl.when(c < passed)
        def _():
            across(c).wait_send()
            across(c).wait_recv()
            for off in range(1, nc):
                along(c, off).wait_send()
                onward(c, off).wait_send()
                onward(c, off).wait_recv()

        return carry

    lax.fori_loop(0, chunks, finish, 0)


def gather(field, n, ny, chunks, passed):
    rows, columns, snapshots, kinds, cells = field.shape
    variables = snapshots * kinds
    width = variables * cells // n
    depth = columns // chunks
    total = n * rows
    nc = ny // 2
    dma = pltpu.SemaphoreType.DMA
    return pl.pallas_call(
        functools.partial(gather_kernel, n, ny, chunks, passed, variables),
        in_specs=[pl.BlockSpec(memory_space=pl.ANY)],
        out_specs=[pl.BlockSpec(memory_space=pl.ANY), pl.BlockSpec(memory_space=pltpu.VMEM)],
        out_shape=[
            jax.ShapeDtypeStruct((ny, columns, total, width), F32),
            jax.ShapeDtypeStruct((total, total), F32),
        ],
        scratch_shapes=[
            pltpu.VMEM((2, cells // LANES, rows, depth * variables, LANES), F32),
            pltpu.VMEM((chunks, n, depth, rows, width), F32),
            pltpu.VMEM((depth, total, width), F32),
            pltpu.VMEM((total, total), F32),
            pltpu.VMEM((total, total), F32),
            dma((chunks, n - 1)),
            dma((chunks, n - 1)),
            dma((chunks,)),
            dma((2, cells // LANES)),
            dma,
            dma((passed, nc - 1)),
            dma((passed, nc - 1)),
            dma((passed,)),
            dma((passed,)),
            dma((passed, nc - 1)),
            dma((passed, nc - 1)),
        ],
        compiler_params=pltpu.CompilerParams(
            collective_id=0, has_side_effects=True, vmem_limit_bytes=VMEM_LIMIT
        ),
    )(field.reshape(rows, columns * variables, cells))


def sum_kernel(nx, ny, p_ref, o_ref, got_y, part, got_x, s1, r1, s2, r2, s3, r3, s4, r4):
    mx, my = lax.axis_index("gx"), lax.axis_index("gy")
    greet("gx", nx)
    greet("gy", ny)
    pl.semaphore_wait(pltpu.get_barrier_semaphore(), nx + ny - 2)

    def push(axis, me, size, source, target, send, recv):
        copies = []
        for off in range(1, size):
            peer = lax.rem(me + off, size)
            copies.append(
                pltpu.make_async_remote_copy(
                    src_ref=source(peer),
                    dst_ref=target(off),
                    send_sem=send.at[off - 1],
                    recv_sem=recv.at[off - 1],
                    device_id={axis: peer},
                    device_id_type=MESH,
                )
            )
        for c in copies:
            c.start()
        return copies

    first = push("gy", my, ny, lambda p: p_ref.at[p], lambda off: got_y.at[off - 1], s1, r1)
    for c in first:
        c.wait_recv()
    total = p_ref[my]
    for off in range(1, ny):
        total = total + got_y[off - 1]
    part[...] = total
    second = push("gx", mx, nx, lambda p: part.at[p], lambda off: got_x.at[off - 1], s2, r2)
    for c in second:
        c.wait_recv()
    total = part[mx]
    for off in range(1, nx):
        total = total + got_x[off - 1]
    o_ref[my, mx] = total
    third = push("gx", mx, nx, lambda p: o_ref.at[my, mx], lambda off: o_ref.at[my, mx], s3, r3)
    for c in third:
        c.wait_recv()
    fourth = push("gy", my, ny, lambda p: o_ref.at[my], lambda off: o_ref.at[my], s4, r4)
    for c in fourth:
        c.wait_recv()
    for c in first + second + third + fourth:
        c.wait_send()


def sum_all(matrix, nx, ny, collective):
    rows, columns = matrix.shape
    small = rows // (nx * ny)
    blocks = matrix.reshape(ny, nx, small, columns)
    out = pl.pallas_call(
        functools.partial(sum_kernel, nx, ny),
        in_specs=[pl.BlockSpec(memory_space=pltpu.VMEM)],
        out_specs=pl.BlockSpec(memory_space=pltpu.VMEM),
        out_shape=jax.ShapeDtypeStruct(blocks.shape, F32),
        scratch_shapes=[
            pltpu.VMEM((ny - 1, nx, small, columns), F32),
            pltpu.VMEM((nx, small, columns), F32),
            pltpu.VMEM((nx - 1, small, columns), F32),
        ]
        + [pltpu.SemaphoreType.DMA((k - 1,)) for k in (ny, ny, nx, nx, nx, nx, ny, ny)],
        compiler_params=pltpu.CompilerParams(
            collective_id=collective, has_side_effects=True, vmem_limit_bytes=VMEM_LIMIT
        ),
    )(blocks)
    return out.reshape(rows, columns)


def reduce_kernel(
    n, chunks, passed, v_ref, f_ref, r_ref, ft, buf, out, pbuf, pout,
    send, recv, own, load, pload, pstore,
):
    me = lax.axis_index("gy")
    columns = v_ref.shape[1]
    depth = columns // chunks
    ranks = r_ref.shape[1]
    left = chunks - passed
    piece = pbuf.shape[1]
    pieces = passed * depth // piece
    greet("gy", n)
    pl.semaphore_wait(pltpu.get_barrier_semaphore(), n - 1)

    def fetch(c):
        return pltpu.make_async_copy(
            v_ref.at[me, pl.ds((passed + c) * depth, depth)],
            buf.at[pl.ds(c * depth, depth)],
            load.at[c],
        )

    def rest(c):
        return pl.ds(me * columns + (passed + c) * depth, depth)

    def copy(c, off):
        peer = lax.rem(me + off, n)
        return pltpu.make_async_remote_copy(
            src_ref=out.at[pl.ds(c * depth, depth), pl.ds(peer * ranks, ranks)],
            dst_ref=r_ref.at[rest(c)],
            send_sem=send.at[c, off - 1],
            recv_sem=recv.at[c, off - 1],
            device_id={"gy": peer},
            device_id_type=MESH,
        )

    def keep(c):
        return pltpu.make_async_copy(
            out.at[pl.ds(c * depth, depth), pl.ds(me * ranks, ranks)],
            r_ref.at[rest(c)],
            own.at[c],
        )

    def pfetch(t):
        slot = lax.rem(t, 2)
        return pltpu.make_async_copy(
            v_ref.at[t // pieces, pl.ds(lax.rem(t, pieces) * piece, piece)],
            pbuf.at[slot],
            pload.at[slot],
        )

    def pkeep(t):
        slot = lax.rem(t, 2)
        return pltpu.make_async_copy(
            pout.at[slot],
            r_ref.at[pl.ds(t // pieces * columns + lax.rem(t, pieces) * piece, piece)],
            pstore.at[slot],
        )

    for c in range(left):
        fetch(c).start()
    pfetch(0).start()
    ft[...] = f_ref[...].T
    factor = split(ft[...])

    def work(c, carry):
        fetch(c).wait()

        def one(j, carry):
            out[c * depth + j] = product(factor, split(buf[c * depth + j]), NN)
            return carry

        lax.fori_loop(0, depth, one, 0)
        for off in range(1, n):
            copy(c, off).start()
        keep(c).start()
        return carry

    lax.fori_loop(0, left, work, 0)
    high, low = split(ft[pl.ds(pl.multiple_of(me * ranks, ranks), ranks), :])
    both = jnp.concatenate([high, low], axis=0)

    def mine(t, carry):
        slot = lax.rem(t, 2)

        @pl.when(t + 1 < n * pieces)
        def _():
            pfetch(t + 1).start()

        pfetch(t).wait()

        @pl.when(t >= 2)
        def _():
            pkeep(t - 2).wait()

        for j in range(piece):
            bh, bl = split(pbuf[slot, j])
            top = jnp.dot(both, bh, preferred_element_type=F32)
            cross = jnp.dot(high, bl, preferred_element_type=F32)
            pout[slot, j] = top[:ranks] + (top[ranks:] + cross)
        pkeep(t).start()
        return carry

    lax.fori_loop(0, n * pieces, mine, 0)
    pkeep(n * pieces - 2).wait()
    pkeep(n * pieces - 1).wait()

    def finish(c, carry):
        for off in range(1, n):
            copy(c, off).wait_recv()
            copy(c, off).wait_send()
        keep(c).wait()
        return carry

    lax.fori_loop(0, left, finish, 0)


def reduce_exchange(unfolded, factor, chunks, passed):
    n, columns, rows, width = unfolded.shape
    rank = factor.shape[1]
    left = chunks - passed
    depth = columns // chunks
    piece = passed * depth // 4
    dma = pltpu.SemaphoreType.DMA
    return pl.pallas_call(
        functools.partial(reduce_kernel, n, chunks, passed),
        in_specs=[pl.BlockSpec(memory_space=pl.ANY), pl.BlockSpec(memory_space=pltpu.VMEM)],
        out_specs=pl.BlockSpec(memory_space=pl.ANY),
        out_shape=jax.ShapeDtypeStruct((n * columns, rank // n, width), F32),
        scratch_shapes=[
            pltpu.VMEM((rank, rows), F32),
            pltpu.VMEM((left * depth, rows, width), F32),
            pltpu.VMEM((left * depth, rank, width), F32),
            pltpu.VMEM((2, piece, rows, width), F32),
            pltpu.VMEM((2, piece, rank // n, width), F32),
            dma((left, n - 1)),
            dma((left, n - 1)),
            dma((left,)),
            dma((left,)),
            dma((2,)),
            dma((2,)),
        ],
        compiler_params=pltpu.CompilerParams(
            collective_id=2, has_side_effects=True, vmem_limit_bytes=VMEM_LIMIT
        ),
    )(unfolded, factor)


def rank_slice(refs, r):
    rows = refs[0].shape[0]
    parts = [
        ref.reshape(rows * 8, LANES)[pl.ds(r, rows, stride=8), :] for ref in refs
    ]
    return parts[0] if len(parts) == 1 else jnp.concatenate(parts, axis=1)


def gram_kernel(halves, *refs):
    *x_refs, g_ref, hh, hl = refs
    step = pl.program_id(0)

    @pl.when(step == 0)
    def _():
        hh[...] = jnp.zeros_like(hh)
        hl[...] = jnp.zeros_like(hl)

    for r in range(8):
        high, low = split(rank_slice(x_refs, r))
        hh[...] += lax.dot_general(high, high, NT, preferred_element_type=F32)
        hl[...] += lax.dot_general(high, low, NT, preferred_element_type=F32)

    @pl.when(step == pl.num_programs(0) - 1)
    def _():
        cross = hl[...]
        g_ref[...] = hh[...] + (cross + cross.T)


def half_specs(rows, halves):
    return [
        pl.BlockSpec((rows, 8, LANES), functools.partial(lambda h, r: (0, r, h), h))
        for h in range(halves)
    ]


def gram(reduced):
    rows, ranks, width = reduced.shape
    halves = width // LANES
    return pl.pallas_call(
        functools.partial(gram_kernel, halves),
        grid=(ranks // 8,),
        in_specs=half_specs(rows, halves),
        out_specs=pl.BlockSpec((rows, rows), lambda r: (0, 0)),
        out_shape=jax.ShapeDtypeStruct((rows, rows), F32),
        scratch_shapes=[pltpu.VMEM((rows, rows), F32), pltpu.VMEM((rows, rows), F32)],
        compiler_params=pltpu.CompilerParams(vmem_limit_bytes=VMEM_LIMIT),
    )(*[reduced] * halves)


def core_kernel(halves, *refs):
    *x_refs, f_ref, o_ref = refs
    factor = split(f_ref[...])
    for r in range(8):
        o_ref[r] = product(split(rank_slice(x_refs, r).T), factor, NN)


def core(reduced, factor):
    rows, ranks, width = reduced.shape
    halves = width // LANES
    kept = factor.shape[1]
    return pl.pallas_call(
        functools.partial(core_kernel, halves),
        grid=(ranks // 8,),
        in_specs=half_specs(rows, halves) + [pl.BlockSpec((rows, kept), lambda r: (0, 0))],
        out_specs=pl.BlockSpec((8, width, kept), lambda r: (r, 0, 0)),
        out_shape=jax.ShapeDtypeStruct((ranks, width, kept), F32),
        compiler_params=pltpu.CompilerParams(vmem_limit_bytes=VMEM_LIMIT),
    )(*[reduced] * halves, factor)


def lower_inverse(products):
    size = products.shape[0]
    group = 4
    count = size // 8
    tiles = [products[8 * t : 8 * t + 8, :] for t in range(count)]
    pivots = [None] * count
    lane = lax.broadcasted_iota(jnp.int32, (8, size), 1)
    row = lax.broadcasted_iota(jnp.int32, (8, size), 0)

    def across(tile, k):
        return jnp.broadcast_to(tile[:, k : k + 1], tile.shape)

    def down(tile, r):
        return jnp.broadcast_to(tile[r : r + 1, :], tile.shape)

    for k in range(0, size, group):
        first = k // 8
        columns = [[across(tiles[t], k + s) for t in range(first, count)] for s in range(group)]
        inside = (lane >= k) & (lane < k + group)
        for t in range(first, count):
            eye = jnp.where(lane == row + 8 * t, 1.0, 0.0)
            tiles[t] = jnp.where(inside, eye, tiles[t])
        for s in range(group):
            r = k + s - 8 * first
            pivot = down(columns[s][0], r)
            pivots[first] = (
                pivot if pivots[first] is None else jnp.where(row >= r, pivot, pivots[first])
            )
            inverse = 1.0 / pivot
            factors = [column * inverse for column in columns[s]]
            factors[0] = jnp.where(row > r, factors[0], 0.0)
            for later in range(s + 1, group):
                head = down(columns[later][0], r)
                columns[later] = [c - f * head for c, f in zip(columns[later], factors)]
            head = down(tiles[first], r)
            for t in range(first, count):
                tiles[t] = tiles[t] - factors[t - first] * head
    rows = [
        jnp.where(lane <= row + 8 * t, tiles[t] * lax.rsqrt(pivots[t]), 0.0) for t in range(count)
    ]
    return jnp.concatenate(rows, axis=0)


def subspace_kernel(g_ref, q_ref, o_ref):
    dot = functools.partial(
        lax.dot_general, precision=lax.Precision.HIGHEST, preferred_element_type=F32
    )
    source = q_ref
    for sweep in range(SWEEPS):
        projected = dot(g_ref[...], source[...], NN)
        inverse = lower_inverse(dot(projected, projected, TN))
        o_ref[...] = dot(projected, inverse, NT)
        source = o_ref


def subspace(gram_matrix, basis):
    return pl.pallas_call(
        subspace_kernel,
        in_specs=[pl.BlockSpec(memory_space=pltpu.VMEM)] * 2,
        out_specs=pl.BlockSpec(memory_space=pltpu.VMEM),
        out_shape=jax.ShapeDtypeStruct(basis.shape, F32),
        compiler_params=pltpu.CompilerParams(vmem_limit_bytes=VMEM_LIMIT),
    )(gram_matrix, basis)


def shards(nx, ny, state_field, start_one, start_two):
    snapshots, variables, cells = state_field.shape[2:]
    rank = start_one.shape[1]
    chunks, passed = 16, 12
    unfolded, partial_one = gather(state_field, nx, ny, chunks, passed)
    factor_one = subspace(sum_all(partial_one, nx, ny, 1), start_one)
    reduced = reduce_exchange(unfolded, factor_one, chunks, passed)
    factor_two = subspace(sum_all(gram(reduced), nx, ny, 1), start_two)
    packed = core(reduced, factor_two)
    packed = packed.reshape(rank // ny, snapshots, variables, cells // nx, rank)
    return packed.transpose(0, 4, 1, 2, 3), factor_one, factor_two


def solution(mesh):
    placed = (P("gx", "gy", None, None, None), P(), P())
    return jax.shard_map(
        functools.partial(shards, mesh.shape["gx"], mesh.shape["gy"]),
        mesh=mesh,
        in_specs=placed,
        out_specs=(P("gy", None, None, None, "gx"), P(), P()),
        check_vma=False,
    )
```

```python
import functools

import jax
import jax.numpy as jnp
from jax import lax
from jax.experimental import pallas as pl
from jax.experimental.pallas import tpu as pltpu
from jax.sharding import PartitionSpec as P

SWEEPS = 2
LANES = 128
MESH = pl.DeviceIdType.MESH
F32 = jnp.float32
BF16 = jnp.bfloat16
NT = (((1,), (1,)), ((), ()))
TN = (((0,), (0,)), ((), ()))
NN = (((1,), (0,)), ((), ()))
VMEM_LIMIT = 48 * 1024 * 1024


def split(x):
    high = x.astype(BF16)
    return high, (x - high.astype(F32)).astype(BF16)


def product(a, b, dims):
    (ah, al), (bh, bl) = a, b
    dot = functools.partial(lax.dot_general, dimension_numbers=dims, preferred_element_type=F32)
    return dot(ah, bh) + (dot(ah, bl) + dot(al, bh))


def relayout(width, variables, x_ref, o_ref):
    halves, rows, held, _ = x_ref.shape
    per = LANES // width
    lane = lax.broadcasted_iota(jnp.int32, (8, LANES), 1)

    def body(t, carry):
        j, octet = t // (rows // 8), lax.rem(t, rows // 8)
        for half in range(halves):
            flat = x_ref.at[half].reshape(rows * held, LANES)
            for h in range(variables // per):
                base = octet * 8 * held + j * variables + h * per
                regs = [flat[pl.ds(base + k, 8, stride=held), :] for k in range(per)]
                step = per // 2
                while step:
                    first = (lane // (width * step)) % 2 == 0
                    for k in range(per):
                        if (k // step) % 2 == 0:
                            a, b = regs[k], regs[k + step]
                            regs[k] = jnp.where(first, a, pltpu.roll(b, width * step, 1))
                            regs[k + step] = jnp.where(
                                first, pltpu.roll(a, LANES - width * step, 1), b
                            )
                    step //= 2
                for g in range(per):
                    o_ref[
                        half * per + g,
                        j,
                        pl.ds(pl.multiple_of(octet * 8, 8), 8),
                        h * LANES : (h + 1) * LANES,
                    ] = regs[g]
        return carry

    lax.fori_loop(0, held // variables * (rows // 8), body, 0)


def greet(axis, size):
    me = lax.axis_index(axis)
    barrier = pltpu.get_barrier_semaphore()
    for off in range(1, size):
        pl.semaphore_signal(
            barrier, inc=1, device_id={axis: lax.rem(me + off, size)}, device_id_type=MESH
        )


def order(n):
    return sorted(range(1, n), key=lambda off: abs(2 * off - n))


def gather_kernel(
    n, ny, chunks, passed, window, variables, x_ref, q_ref, v_ref, f_ref,
    xb, ob, buf, hh, hl, send, recv, own, load, fill, xs, xr, bs, br, cs, cr, *adding
):
    me, my = lax.axis_index("gx"), lax.axis_index("gy")
    nc = ny // 2
    place, side = my // 2, lax.rem(my, 2)
    sibling = place * 2 + 1 - side
    depth, rows, width = ob.shape[2:]
    held = depth * variables
    lag = 2

    greet("gx", n)
    greet("gy", ny)
    pl.semaphore_wait(pltpu.get_barrier_semaphore(), n + ny - 2)

    def take(c, half):
        slot = lax.rem(c, 2)
        return pltpu.make_async_copy(
            x_ref.at[:, pl.ds(c * held, held), pl.ds(half * LANES, LANES)],
            xb.at[slot, half],
            load.at[slot, half],
        )

    def span(c):
        return pl.ds(c * depth, depth)

    def copy(c, off):
        peer = lax.rem(me + off, n)
        return pltpu.make_async_remote_copy(
            src_ref=ob.at[c, peer],
            dst_ref=v_ref.at[my, span(c), pl.ds(me * rows, rows)],
            send_sem=send.at[c, off - 1],
            recv_sem=recv.at[c, off - 1],
            device_id={"gx": peer},
            device_id_type=MESH,
        )

    def keep(c):
        return pltpu.make_async_copy(
            ob.at[c, me], v_ref.at[my, span(c), pl.ds(me * rows, rows)], own.at[c]
        )

    def along(c, off):
        return pltpu.make_async_remote_copy(
            src_ref=v_ref.at[my, span(c)],
            dst_ref=v_ref.at[my, span(c)],
            send_sem=xs.at[c, off - 1],
            recv_sem=xr.at[c, off - 1],
            device_id={"gy": lax.rem(place + off, nc) * 2 + side},
            device_id_type=MESH,
        )

    def across(c):
        return pltpu.make_async_remote_copy(
            src_ref=v_ref.at[my, span(c)],
            dst_ref=v_ref.at[my, span(c)],
            send_sem=bs.at[c],
            recv_sem=br.at[c],
            device_id={"gy": sibling},
            device_id_type=MESH,
        )

    def onward(c, off):
        origin = lax.rem(place + nc - off, nc) * 2 + side
        return pltpu.make_async_remote_copy(
            src_ref=v_ref.at[origin, span(c)],
            dst_ref=v_ref.at[origin, span(c)],
            send_sem=cs.at[c, off - 1],
            recv_sem=cr.at[c, off - 1],
            device_id={"gy": sibling},
            device_id_type=MESH,
        )

    halves = xb.shape[1]
    for half in range(halves):
        take(0, half).start()

    def start(c, carry):
        @pl.when(c + 1 < chunks)
        def _():
            for half in range(halves):
                take(c + 1, half).start()

        for half in range(halves):
            take(c, half).wait()
        relayout(width // variables, variables, xb.at[lax.rem(c, 2)], ob.at[c])
        for off in order(n):
            copy(c, off).start()
        keep(c).start()
        return carry

    hh[...] = jnp.zeros_like(hh)
    hl[...] = jnp.zeros_like(hl)

    def work(c, carry):
        for off in range(1, n):
            copy(c, off).wait_recv()
        keep(c).wait()
        fetch = pltpu.make_async_copy(v_ref.at[my, span(c)], buf, fill)
        fetch.start()

        @pl.when(c < passed)
        def _():
            for off in range(1, nc):
                along(c, off).start()
            across(c).start()

        late = c - lag

        @pl.when((late >= 0) & (late < passed))
        def _():
            for off in range(1, nc):
                along(late, off).wait_recv()
                onward(late, off).start()

        fetch.wait()

        def one(j, carry):
            high, low = split(buf[j])
            hh[...] += lax.dot_general(high, high, NT, preferred_element_type=F32)
            hl[...] += lax.dot_general(high, low, NT, preferred_element_type=F32)
            return carry

        lax.fori_loop(0, depth, one, 0)
        return carry

    def turn(t, carry):
        @pl.when(t < chunks)
        def _():
            start(t, 0)

        @pl.when(t >= window)
        def _():
            work(t - window, 0)

        return carry

    lax.fori_loop(0, chunks + window, turn, 0)
    cross = hl[...]
    adding[0][...] = hh[...] + (cross + cross.T)
    sum_devices(n, ny, *adding)
    subspace_steps(adding[1], q_ref, f_ref)

    def finish(c, carry):
        for off in range(1, n):
            copy(c, off).wait_send()

        @pl.when(c < passed)
        def _():
            across(c).wait_send()
            across(c).wait_recv()
            for off in range(1, nc):
                along(c, off).wait_send()
                onward(c, off).wait_send()
                onward(c, off).wait_recv()

        return carry

    lax.fori_loop(0, chunks, finish, 0)


def gather(field, start, n, ny, chunks, passed, window):
    rows, columns, snapshots, kinds, cells = field.shape
    variables = snapshots * kinds
    width = variables * cells // n
    depth = columns // chunks
    total = n * rows
    nc = ny // 2
    dma = pltpu.SemaphoreType.DMA
    return pl.pallas_call(
        functools.partial(gather_kernel, n, ny, chunks, passed, window, variables),
        in_specs=[pl.BlockSpec(memory_space=pl.ANY), pl.BlockSpec(memory_space=pltpu.VMEM)],
        out_specs=[pl.BlockSpec(memory_space=pl.ANY), pl.BlockSpec(memory_space=pltpu.VMEM)],
        out_shape=[
            jax.ShapeDtypeStruct((ny, columns, total, width), F32),
            jax.ShapeDtypeStruct(start.shape, F32),
        ],
        scratch_shapes=[
            pltpu.VMEM((2, cells // LANES, rows, depth * variables, LANES), F32),
            pltpu.VMEM((chunks, n, depth, rows, width), F32),
            pltpu.VMEM((depth, total, width), F32),
            pltpu.VMEM((total, total), F32),
            pltpu.VMEM((total, total), F32),
            dma((chunks, n - 1)),
            dma((chunks, n - 1)),
            dma((chunks,)),
            dma((2, cells // LANES)),
            dma,
            dma((passed, nc - 1)),
            dma((passed, nc - 1)),
            dma((passed,)),
            dma((passed,)),
            dma((passed, nc - 1)),
            dma((passed, nc - 1)),
        ]
        + sum_scratch(total, n, ny),
        compiler_params=pltpu.CompilerParams(
            collective_id=0, has_side_effects=True, vmem_limit_bytes=VMEM_LIMIT
        ),
    )(field.reshape(rows, columns * variables, cells), start)


def sum_scratch(size, nx, ny):
    rows = size // ny
    small = rows // nx
    got = (nx - 1, small, size) if small % 8 == 0 else (nx, rows, size)
    return [
        pltpu.VMEM((size, size), F32),
        pltpu.VMEM((size, size), F32),
        pltpu.VMEM((ny - 1, rows, size), F32),
        pltpu.VMEM((rows, size), F32),
        pltpu.VMEM(got, F32),
    ] + [pltpu.SemaphoreType.DMA((k - 1,)) for k in (ny, ny, nx, nx, nx, nx, ny, ny)]


def sum_devices(nx, ny, part, total, got_y, held, got_x, s1, r1, s2, r2, s3, r3, s4, r4):
    mx, my = lax.axis_index("gx"), lax.axis_index("gy")
    rows = part.shape[0] // ny
    small = rows // nx

    def push(axis, me, size, source, target, send, recv):
        copies = []
        for off in range(1, size):
            peer = lax.rem(me + off, size)
            copies.append(
                pltpu.make_async_remote_copy(
                    src_ref=source(peer),
                    dst_ref=target(off),
                    send_sem=send.at[off - 1],
                    recv_sem=recv.at[off - 1],
                    device_id={axis: peer},
                    device_id_type=MESH,
                )
            )
        for c in copies:
            c.start()
        for c in copies:
            c.wait_recv()
        return copies

    def slab(p):
        return pl.ds(pl.multiple_of(p * rows, 8), rows)

    sent = push("gy", my, ny, lambda p: part.at[slab(p)], lambda off: got_y.at[off - 1], s1, r1)
    value = part[slab(my), :]
    for off in range(1, ny):
        value = value + got_y[off - 1]
    held[...] = value
    if small % 8 == 0:
        def strip(p):
            return pl.ds(pl.multiple_of(p * small, 8), small)

        sent += push(
            "gx", mx, nx, lambda p: held.at[strip(p)], lambda off: got_x.at[off - 1], s2, r2
        )
        value = held[strip(mx), :]
        for off in range(1, nx):
            value = value + got_x[off - 1]
        own = pl.ds(pl.multiple_of(my * rows + mx * small, 8), small)
        total[own, :] = value
        sent += push("gx", mx, nx, lambda p: total.at[own], lambda off: total.at[own], s3, r3)
    else:
        got_x[mx] = value
        sent += push("gx", mx, nx, lambda p: held, lambda off: got_x.at[mx], s2, r2)
        value = got_x[0]
        for p in range(1, nx):
            value = value + got_x[p]
        total[slab(my), :] = value
    sent += push(
        "gy", my, ny, lambda p: total.at[slab(my)], lambda off: total.at[slab(my)], s4, r4
    )
    for c in sent:
        c.wait_send()


def reduce_kernel(
    nx, n, chunks, passed, v_ref, f_ref, q_ref, o_ref, f2_ref, ft, buf, out, pbuf, red, hh, hl,
    send, recv, own, load, pload, store, *adding
):
    me = lax.axis_index("gy")
    columns = v_ref.shape[1]
    depth = columns // chunks
    halves, rows, ranks, _ = red.shape
    left = chunks - passed
    piece = pbuf.shape[1]
    pieces = passed * depth // piece
    greet("gx", nx)
    greet("gy", n)

    def fetch(c):
        return pltpu.make_async_copy(
            v_ref.at[me, pl.ds((passed + c) * depth, depth)],
            buf.at[pl.ds(c * depth, depth)],
            load.at[c],
        )

    def rest(c):
        return pl.ds(me * columns + (passed + c) * depth, depth)

    def copy(c, off):
        peer = lax.rem(me + off, n)
        return pltpu.make_async_remote_copy(
            src_ref=out.at[:, pl.ds(c * depth, depth), pl.ds(peer * ranks, ranks)],
            dst_ref=red.at[:, rest(c)],
            send_sem=send.at[c, off - 1],
            recv_sem=recv.at[c, off - 1],
            device_id={"gy": peer},
            device_id_type=MESH,
        )

    def keep(c):
        return pltpu.make_async_copy(
            out.at[:, pl.ds(c * depth, depth), pl.ds(me * ranks, ranks)],
            red.at[:, rest(c)],
            own.at[c],
        )

    def pfetch(t):
        slot = lax.rem(t, 2)
        return pltpu.make_async_copy(
            v_ref.at[t // pieces, pl.ds(lax.rem(t, pieces) * piece, piece)],
            pbuf.at[slot],
            pload.at[slot],
        )

    for c in range(left):
        fetch(c).start()
    pfetch(0).start()
    ft[...] = f_ref[...].T
    factor = split(ft[...])
    pl.semaphore_wait(pltpu.get_barrier_semaphore(), nx + n - 2)

    def work(c, carry):
        fetch(c).wait()

        def one(j, carry):
            value = product(factor, split(buf[c * depth + j]), NN)
            for h in range(halves):
                out[h, c * depth + j] = value[:, h * LANES : (h + 1) * LANES]
            return carry

        lax.fori_loop(0, depth, one, 0)
        for off in range(1, n):
            copy(c, off).start()
        keep(c).start()
        return carry

    lax.fori_loop(0, left, work, 0)
    high, low = split(ft[pl.ds(pl.multiple_of(me * ranks, ranks), ranks), :])
    both = jnp.concatenate([high, low], axis=0)

    def mine(t, carry):
        slot = lax.rem(t, 2)

        @pl.when(t + 1 < n * pieces)
        def _():
            pfetch(t + 1).start()

        pfetch(t).wait()
        first = t // pieces * columns + lax.rem(t, pieces) * piece
        for j in range(piece):
            bh, bl = split(pbuf[slot, j])
            top = jnp.dot(both, bh, preferred_element_type=F32)
            cross = jnp.dot(high, bl, preferred_element_type=F32)
            value = top[:ranks] + (top[ranks:] + cross)
            for h in range(halves):
                red[h, first + j] = value[:, h * LANES : (h + 1) * LANES]
        return carry

    lax.fori_loop(0, n * pieces, mine, 0)

    def finish(c, carry):
        for off in range(1, n):
            copy(c, off).wait_recv()
            copy(c, off).wait_send()
        keep(c).wait()
        return carry

    lax.fori_loop(0, left, finish, 0)
    away = pltpu.make_async_copy(red, o_ref, store)
    away.start()
    hh[...] = jnp.zeros_like(hh)
    hl[...] = jnp.zeros_like(hl)

    def gram(g, carry):
        for k in range(4):
            parts = [
                red.at[h].reshape(rows * ranks, LANES)[pl.ds(g * 4 + k, rows, stride=ranks), :]
                for h in range(halves)
            ]
            high, low = split(parts[0] if halves == 1 else jnp.concatenate(parts, axis=1))
            hh[...] += lax.dot_general(high, high, NT, preferred_element_type=F32)
            hl[...] += lax.dot_general(high, low, NT, preferred_element_type=F32)
        return carry

    lax.fori_loop(0, ranks // 4, gram, 0)
    cross = hl[...]
    adding[0][...] = hh[...] + (cross + cross.T)
    sum_devices(nx, n, *adding)
    subspace_steps(adding[1], q_ref, f2_ref)
    away.wait()


def reduce_exchange(unfolded, factor, start, nx, chunks, passed):
    n, columns, rows, width = unfolded.shape
    rank = factor.shape[1]
    left = chunks - passed
    depth = columns // chunks
    piece = passed * depth // 4
    size = n * columns
    halves = width // LANES
    dma = pltpu.SemaphoreType.DMA
    return pl.pallas_call(
        functools.partial(reduce_kernel, nx, n, chunks, passed),
        in_specs=[pl.BlockSpec(memory_space=pl.ANY)]
        + [pl.BlockSpec(memory_space=pltpu.VMEM)] * 2,
        out_specs=[pl.BlockSpec(memory_space=pl.ANY), pl.BlockSpec(memory_space=pltpu.VMEM)],
        out_shape=[
            jax.ShapeDtypeStruct((halves, size, rank // n, LANES), F32),
            jax.ShapeDtypeStruct(start.shape, F32),
        ],
        scratch_shapes=[
            pltpu.VMEM((rank, rows), F32),
            pltpu.VMEM((left * depth, rows, width), F32),
            pltpu.VMEM((halves, left * depth, rank, LANES), F32),
            pltpu.VMEM((2, piece, rows, width), F32),
            pltpu.VMEM((halves, size, rank // n, LANES), F32),
            pltpu.VMEM((size, size), F32),
            pltpu.VMEM((size, size), F32),
            dma((left, n - 1)),
            dma((left, n - 1)),
            dma((left,)),
            dma((left,)),
            dma((2,)),
            dma,
        ]
        + sum_scratch(size, nx, n),
        compiler_params=pltpu.CompilerParams(
            collective_id=1, has_side_effects=True, vmem_limit_bytes=VMEM_LIMIT
        ),
    )(unfolded, factor, start)


def core_kernel(halves, *refs):
    *x_refs, f_ref, o_ref = refs
    factor = split(f_ref[...])
    rows = f_ref.shape[0]
    for r in range(8):
        parts = [
            ref.at[0].reshape(rows * 8, LANES)[pl.ds(r, rows, stride=8), :] for ref in x_refs
        ]
        values = parts[0] if halves == 1 else jnp.concatenate(parts, axis=1)
        o_ref[r] = product(split(values.T), factor, NN)


def core(reduced, factor):
    halves, rows, ranks, _ = reduced.shape
    width = halves * LANES
    kept = factor.shape[1]
    specs = [
        pl.BlockSpec((1, rows, 8, LANES), functools.partial(lambda h, r: (h, 0, r, 0), h))
        for h in range(halves)
    ]
    return pl.pallas_call(
        functools.partial(core_kernel, halves),
        grid=(ranks // 8,),
        in_specs=specs + [pl.BlockSpec((rows, kept), lambda r: (0, 0))],
        out_specs=pl.BlockSpec((8, width, kept), lambda r: (r, 0, 0)),
        out_shape=jax.ShapeDtypeStruct((ranks, width, kept), F32),
        compiler_params=pltpu.CompilerParams(vmem_limit_bytes=VMEM_LIMIT),
    )(*[reduced] * halves, factor)


def lower_inverse(products):
    size = products.shape[0]
    group = 4
    count = size // 8
    tiles = [products[8 * t : 8 * t + 8, :] for t in range(count)]
    pivots = [None] * count
    lane = lax.broadcasted_iota(jnp.int32, (8, size), 1)
    row = lax.broadcasted_iota(jnp.int32, (8, size), 0)

    def across(tile, k):
        return jnp.broadcast_to(tile[:, k : k + 1], tile.shape)

    def down(tile, r):
        return jnp.broadcast_to(tile[r : r + 1, :], tile.shape)

    for k in range(0, size, group):
        first = k // 8
        columns = [[across(tiles[t], k + s) for t in range(first, count)] for s in range(group)]
        inside = (lane >= k) & (lane < k + group)
        for t in range(first, count):
            eye = jnp.where(lane == row + 8 * t, 1.0, 0.0)
            tiles[t] = jnp.where(inside, eye, tiles[t])
        for s in range(group):
            r = k + s - 8 * first
            pivot = down(columns[s][0], r)
            pivots[first] = (
                pivot if pivots[first] is None else jnp.where(row >= r, pivot, pivots[first])
            )
            inverse = 1.0 / pivot
            factors = [column * inverse for column in columns[s]]
            factors[0] = jnp.where(row > r, factors[0], 0.0)
            for later in range(s + 1, group):
                head = down(columns[later][0], r)
                columns[later] = [c - f * head for c, f in zip(columns[later], factors)]
            head = down(tiles[first], r)
            for t in range(first, count):
                tiles[t] = tiles[t] - factors[t - first] * head
    rows = [
        jnp.where(lane <= row + 8 * t, tiles[t] * lax.rsqrt(pivots[t]), 0.0) for t in range(count)
    ]
    return jnp.concatenate(rows, axis=0)


def subspace_steps(g_ref, q_ref, o_ref):
    dot = functools.partial(
        lax.dot_general, precision=lax.Precision.HIGHEST, preferred_element_type=F32
    )
    source = q_ref
    for sweep in range(SWEEPS):
        projected = dot(g_ref[...], source[...], NN)
        inverse = lower_inverse(dot(projected, projected, TN))
        o_ref[...] = dot(projected, inverse, NT)
        source = o_ref


def shards(nx, ny, state_field, start_one, start_two):
    snapshots, variables, cells = state_field.shape[2:]
    rank = start_one.shape[1]
    chunks, passed, window = 16, 12, 4
    unfolded, factor_one = gather(state_field, start_one, nx, ny, chunks, passed, window)
    reduced, factor_two = reduce_exchange(unfolded, factor_one, start_two, nx, chunks, passed)
    packed = core(reduced, factor_two)
    packed = packed.reshape(rank // ny, snapshots, variables, cells // nx, rank)
    return packed.transpose(0, 4, 1, 2, 3), factor_one, factor_two


def solution(mesh):
    placed = (P("gx", "gy", None, None, None), P(), P())
    return jax.shard_map(
        functools.partial(shards, mesh.shape["gx"], mesh.shape["gy"]),
        mesh=mesh,
        in_specs=placed,
        out_specs=(P("gy", None, None, None, "gx"), P(), P()),
        check_vma=False,
    )
```

```python
import functools

import jax
import jax.numpy as jnp
from jax import lax
from jax.experimental import pallas as pl
from jax.experimental.pallas import tpu as pltpu
from jax.sharding import PartitionSpec as P

SWEEPS = 2
LANES = 128
MESH = pl.DeviceIdType.MESH
F32 = jnp.float32
BF16 = jnp.bfloat16
NT = (((1,), (1,)), ((), ()))
TN = (((0,), (0,)), ((), ()))
NN = (((1,), (0,)), ((), ()))
VMEM_LIMIT = 48 * 1024 * 1024


def split(x):
    high = x.astype(BF16)
    return high, (x - high.astype(F32)).astype(BF16)


def product(a, b, dims):
    (ah, al), (bh, bl) = a, b
    dot = functools.partial(lax.dot_general, dimension_numbers=dims, preferred_element_type=F32)
    return dot(ah, bh) + (dot(ah, bl) + dot(al, bh))


def relayout(width, variables, x_ref, o_ref):
    halves, rows, held, _ = x_ref.shape
    per = LANES // width
    lane = lax.broadcasted_iota(jnp.int32, (8, LANES), 1)

    def body(t, carry):
        j, octet = t // (rows // 8), lax.rem(t, rows // 8)
        for half in range(halves):
            flat = x_ref.at[half].reshape(rows * held, LANES)
            for h in range(variables // per):
                base = octet * 8 * held + j * variables + h * per
                regs = [flat[pl.ds(base + k, 8, stride=held), :] for k in range(per)]
                step = per // 2
                while step:
                    first = (lane // (width * step)) % 2 == 0
                    for k in range(per):
                        if (k // step) % 2 == 0:
                            a, b = regs[k], regs[k + step]
                            regs[k] = jnp.where(first, a, pltpu.roll(b, width * step, 1))
                            regs[k + step] = jnp.where(
                                first, pltpu.roll(a, LANES - width * step, 1), b
                            )
                    step //= 2
                for g in range(per):
                    o_ref[
                        half * per + g,
                        j,
                        pl.ds(pl.multiple_of(octet * 8, 8), 8),
                        h * LANES : (h + 1) * LANES,
                    ] = regs[g]
        return carry

    lax.fori_loop(0, held // variables * (rows // 8), body, 0)


def greet(axis, size):
    me = lax.axis_index(axis)
    barrier = pltpu.get_barrier_semaphore()
    for off in range(1, size):
        pl.semaphore_signal(
            barrier, inc=1, device_id={axis: lax.rem(me + off, size)}, device_id_type=MESH
        )


def order(n):
    return sorted(range(1, n), key=lambda off: abs(2 * off - n))


def gather_kernel(
    n, ny, chunks, passed, window, variables, x_ref, q_ref, v_ref, f_ref,
    xb, ob, buf, hh, hl, send, recv, own, load, fill, xs, xr, bs, br, cs, cr, *adding
):
    me, my = lax.axis_index("gx"), lax.axis_index("gy")
    nc = ny // 2
    place, side = my // 2, lax.rem(my, 2)
    sibling = place * 2 + 1 - side
    depth, rows, width = ob.shape[2:]
    held = depth * variables
    lag = 2

    greet("gx", n)
    greet("gy", ny)
    pl.semaphore_wait(pltpu.get_barrier_semaphore(), n + ny - 2)

    def take(c, half):
        slot = lax.rem(c, 2)
        return pltpu.make_async_copy(
            x_ref.at[:, pl.ds(c * held, held), pl.ds(half * LANES, LANES)],
            xb.at[slot, half],
            load.at[slot, half],
        )

    def span(c):
        return pl.ds(c * depth, depth)

    def copy(c, off):
        peer = lax.rem(me + off, n)
        return pltpu.make_async_remote_copy(
            src_ref=ob.at[c, peer],
            dst_ref=v_ref.at[my, span(c), pl.ds(me * rows, rows)],
            send_sem=send.at[c, off - 1],
            recv_sem=recv.at[c, off - 1],
            device_id={"gx": peer},
            device_id_type=MESH,
        )

    def keep(c):
        return pltpu.make_async_copy(
            ob.at[c, me], v_ref.at[my, span(c), pl.ds(me * rows, rows)], own.at[c]
        )

    def along(c, off):
        return pltpu.make_async_remote_copy(
            src_ref=v_ref.at[my, span(c)],
            dst_ref=v_ref.at[my, span(c)],
            send_sem=xs.at[c, off - 1],
            recv_sem=xr.at[c, off - 1],
            device_id={"gy": lax.rem(place + off, nc) * 2 + side},
            device_id_type=MESH,
        )

    def across(c):
        return pltpu.make_async_remote_copy(
            src_ref=v_ref.at[my, span(c)],
            dst_ref=v_ref.at[my, span(c)],
            send_sem=bs.at[c],
            recv_sem=br.at[c],
            device_id={"gy": sibling},
            device_id_type=MESH,
        )

    def onward(c, off):
        origin = lax.rem(place + nc - off, nc) * 2 + side
        return pltpu.make_async_remote_copy(
            src_ref=v_ref.at[origin, span(c)],
            dst_ref=v_ref.at[origin, span(c)],
            send_sem=cs.at[c, off - 1],
            recv_sem=cr.at[c, off - 1],
            device_id={"gy": sibling},
            device_id_type=MESH,
        )

    halves = xb.shape[1]
    for half in range(halves):
        take(0, half).start()

    def start(c, carry):
        @pl.when(c + 1 < chunks)
        def _():
            for half in range(halves):
                take(c + 1, half).start()

        for half in range(halves):
            take(c, half).wait()
        relayout(width // variables, variables, xb.at[lax.rem(c, 2)], ob.at[c])
        for off in order(n):
            copy(c, off).start()
        keep(c).start()
        return carry

    hh[...] = jnp.zeros_like(hh)
    hl[...] = jnp.zeros_like(hl)

    def work(c, carry):
        for off in range(1, n):
            copy(c, off).wait_recv()
        keep(c).wait()
        fetch = pltpu.make_async_copy(v_ref.at[my, span(c)], buf, fill)
        fetch.start()

        @pl.when(c < passed)
        def _():
            for off in range(1, nc):
                along(c, off).start()
            across(c).start()

        late = c - lag

        @pl.when((late >= 0) & (late < passed))
        def _():
            for off in range(1, nc):
                along(late, off).wait_recv()
                onward(late, off).start()

        fetch.wait()

        def one(j, carry):
            high, low = split(buf[j])
            hh[...] += lax.dot_general(high, high, NT, preferred_element_type=F32)
            hl[...] += lax.dot_general(high, low, NT, preferred_element_type=F32)
            return carry

        lax.fori_loop(0, depth, one, 0)
        return carry

    def turn(t, carry):
        @pl.when(t < chunks)
        def _():
            start(t, 0)

        @pl.when(t >= window)
        def _():
            work(t - window, 0)

        return carry

    lax.fori_loop(0, chunks + window, turn, 0)
    cross = hl[...]
    adding[0][...] = hh[...] + (cross + cross.T)
    sum_devices(n, ny, *adding)
    subspace_steps(adding[1], q_ref, f_ref)

    def finish(c, carry):
        for off in range(1, n):
            copy(c, off).wait_send()

        @pl.when(c < passed)
        def _():
            across(c).wait_send()
            across(c).wait_recv()
            for off in range(1, nc):
                along(c, off).wait_send()
                onward(c, off).wait_send()
                onward(c, off).wait_recv()

        return carry

    lax.fori_loop(0, chunks, finish, 0)


def gather(field, start, n, ny, chunks, passed, window):
    rows, columns, snapshots, kinds, cells = field.shape
    variables = snapshots * kinds
    width = variables * cells // n
    depth = columns // chunks
    total = n * rows
    nc = ny // 2
    dma = pltpu.SemaphoreType.DMA
    return pl.pallas_call(
        functools.partial(gather_kernel, n, ny, chunks, passed, window, variables),
        in_specs=[pl.BlockSpec(memory_space=pl.ANY), pl.BlockSpec(memory_space=pltpu.VMEM)],
        out_specs=[pl.BlockSpec(memory_space=pl.ANY), pl.BlockSpec(memory_space=pltpu.VMEM)],
        out_shape=[
            jax.ShapeDtypeStruct((ny, columns, total, width), F32),
            jax.ShapeDtypeStruct(start.shape, F32),
        ],
        scratch_shapes=[
            pltpu.VMEM((2, cells // LANES, rows, depth * variables, LANES), F32),
            pltpu.VMEM((chunks, n, depth, rows, width), F32),
            pltpu.VMEM((depth, total, width), F32),
            pltpu.VMEM((total, total), F32),
            pltpu.VMEM((total, total), F32),
            dma((chunks, n - 1)),
            dma((chunks, n - 1)),
            dma((chunks,)),
            dma((2, cells // LANES)),
            dma,
            dma((passed, nc - 1)),
            dma((passed, nc - 1)),
            dma((passed,)),
            dma((passed,)),
            dma((passed, nc - 1)),
            dma((passed, nc - 1)),
        ]
        + sum_scratch(total, n, ny),
        compiler_params=pltpu.CompilerParams(
            collective_id=0, has_side_effects=True, vmem_limit_bytes=VMEM_LIMIT
        ),
    )(field.reshape(rows, columns * variables, cells), start)


def sum_scratch(size, nx, ny):
    rows = size // ny
    small = rows // nx
    got = (nx - 1, small, size) if small % 8 == 0 else (nx, rows, size)
    return [
        pltpu.VMEM((size, size), F32),
        pltpu.VMEM((size, size), F32),
        pltpu.VMEM((ny - 1, rows, size), F32),
        pltpu.VMEM((rows, size), F32),
        pltpu.VMEM(got, F32),
    ] + [pltpu.SemaphoreType.DMA((k - 1,)) for k in (ny, ny, nx, nx, nx, nx, ny, ny)]


def sum_devices(nx, ny, part, total, got_y, held, got_x, s1, r1, s2, r2, s3, r3, s4, r4):
    mx, my = lax.axis_index("gx"), lax.axis_index("gy")
    rows = part.shape[0] // ny
    small = rows // nx

    def push(axis, me, size, source, target, send, recv):
        copies = []
        for off in range(1, size):
            peer = lax.rem(me + off, size)
            copies.append(
                pltpu.make_async_remote_copy(
                    src_ref=source(peer),
                    dst_ref=target(off),
                    send_sem=send.at[off - 1],
                    recv_sem=recv.at[off - 1],
                    device_id={axis: peer},
                    device_id_type=MESH,
                )
            )
        for c in copies:
            c.start()
        for c in copies:
            c.wait_recv()
        return copies

    def slab(p):
        return pl.ds(pl.multiple_of(p * rows, 8), rows)

    sent = push("gy", my, ny, lambda p: part.at[slab(p)], lambda off: got_y.at[off - 1], s1, r1)
    value = part[slab(my), :]
    for off in range(1, ny):
        value = value + got_y[off - 1]
    held[...] = value
    if small % 8 == 0:
        def strip(p):
            return pl.ds(pl.multiple_of(p * small, 8), small)

        sent += push(
            "gx", mx, nx, lambda p: held.at[strip(p)], lambda off: got_x.at[off - 1], s2, r2
        )
        value = held[strip(mx), :]
        for off in range(1, nx):
            value = value + got_x[off - 1]
        own = pl.ds(pl.multiple_of(my * rows + mx * small, 8), small)
        total[own, :] = value
        sent += push("gx", mx, nx, lambda p: total.at[own], lambda off: total.at[own], s3, r3)
    else:
        got_x[mx] = value
        sent += push("gx", mx, nx, lambda p: held, lambda off: got_x.at[mx], s2, r2)
        value = got_x[0]
        for p in range(1, nx):
            value = value + got_x[p]
        total[slab(my), :] = value
    sent += push(
        "gy", my, ny, lambda p: total.at[slab(my)], lambda off: total.at[slab(my)], s4, r4
    )
    for c in sent:
        c.wait_send()


def reduce_kernel(
    nx, n, chunks, passed, v_ref, f_ref, q_ref, o_ref, f2_ref, ft, buf, out, pbuf, red, hh, hl,
    send, recv, own, load, pload, store, *adding
):
    me = lax.axis_index("gy")
    columns = v_ref.shape[1]
    depth = columns // chunks
    halves, rows, ranks, _ = red.shape
    left = chunks - passed
    piece = pbuf.shape[1]
    pieces = passed * depth // piece
    greet("gx", nx)
    greet("gy", n)

    def fetch(c):
        return pltpu.make_async_copy(
            v_ref.at[me, pl.ds((passed + c) * depth, depth)],
            buf.at[pl.ds(c * depth, depth)],
            load.at[c],
        )

    def rest(c):
        return pl.ds(me * columns + (passed + c) * depth, depth)

    def copy(c, off):
        peer = lax.rem(me + off, n)
        return pltpu.make_async_remote_copy(
            src_ref=out.at[:, pl.ds(c * depth, depth), pl.ds(peer * ranks, ranks)],
            dst_ref=red.at[:, rest(c)],
            send_sem=send.at[c, off - 1],
            recv_sem=recv.at[c, off - 1],
            device_id={"gy": peer},
            device_id_type=MESH,
        )

    def keep(c):
        return pltpu.make_async_copy(
            out.at[:, pl.ds(c * depth, depth), pl.ds(me * ranks, ranks)],
            red.at[:, rest(c)],
            own.at[c],
        )

    def pfetch(t):
        slot = lax.rem(t, 2)
        return pltpu.make_async_copy(
            v_ref.at[t // pieces, pl.ds(lax.rem(t, pieces) * piece, piece)],
            pbuf.at[slot],
            pload.at[slot],
        )

    for c in range(left):
        fetch(c).start()
    pfetch(0).start()
    ft[...] = f_ref[...].T
    factor = split(ft[...])
    pl.semaphore_wait(pltpu.get_barrier_semaphore(), nx + n - 2)

    def work(c, carry):
        fetch(c).wait()

        def one(j, carry):
            value = product(factor, split(buf[c * depth + j]), NN)
            for h in range(halves):
                out[h, c * depth + j] = value[:, h * LANES : (h + 1) * LANES]
            return carry

        lax.fori_loop(0, depth, one, 0)
        for off in range(1, n):
            copy(c, off).start()
        keep(c).start()
        return carry

    lax.fori_loop(0, left, work, 0)
    high, low = split(ft[pl.ds(pl.multiple_of(me * ranks, ranks), ranks), :])
    both = jnp.concatenate([high, low], axis=0)

    def mine(t, carry):
        slot = lax.rem(t, 2)

        @pl.when(t + 1 < n * pieces)
        def _():
            pfetch(t + 1).start()

        pfetch(t).wait()
        first = t // pieces * columns + lax.rem(t, pieces) * piece
        for j in range(piece):
            bh, bl = split(pbuf[slot, j])
            top = jnp.dot(both, bh, preferred_element_type=F32)
            cross = jnp.dot(high, bl, preferred_element_type=F32)
            value = top[:ranks] + (top[ranks:] + cross)
            for h in range(halves):
                red[h, first + j] = value[:, h * LANES : (h + 1) * LANES]
        return carry

    lax.fori_loop(0, n * pieces, mine, 0)

    def finish(c, carry):
        for off in range(1, n):
            copy(c, off).wait_recv()
            copy(c, off).wait_send()
        keep(c).wait()
        return carry

    lax.fori_loop(0, left, finish, 0)
    away = pltpu.make_async_copy(red, o_ref, store)
    away.start()
    hh[...] = jnp.zeros_like(hh)
    hl[...] = jnp.zeros_like(hl)

    def gram(g, carry):
        for k in range(4):
            parts = [
                red.at[h].reshape(rows * ranks, LANES)[pl.ds(g * 4 + k, rows, stride=ranks), :]
                for h in range(halves)
            ]
            high, low = split(parts[0] if halves == 1 else jnp.concatenate(parts, axis=1))
            hh[...] += lax.dot_general(high, high, NT, preferred_element_type=F32)
            hl[...] += lax.dot_general(high, low, NT, preferred_element_type=F32)
        return carry

    lax.fori_loop(0, ranks // 4, gram, 0)
    cross = hl[...]
    adding[0][...] = hh[...] + (cross + cross.T)
    sum_devices(nx, n, *adding)
    subspace_steps(adding[1], q_ref, f2_ref)
    away.wait()


def reduce_exchange(unfolded, factor, start, nx, chunks, passed):
    n, columns, rows, width = unfolded.shape
    rank = factor.shape[1]
    left = chunks - passed
    depth = columns // chunks
    piece = passed * depth // 4
    size = n * columns
    halves = width // LANES
    dma = pltpu.SemaphoreType.DMA
    return pl.pallas_call(
        functools.partial(reduce_kernel, nx, n, chunks, passed),
        in_specs=[pl.BlockSpec(memory_space=pl.ANY)]
        + [pl.BlockSpec(memory_space=pltpu.VMEM)] * 2,
        out_specs=[pl.BlockSpec(memory_space=pl.ANY), pl.BlockSpec(memory_space=pltpu.VMEM)],
        out_shape=[
            jax.ShapeDtypeStruct((halves, size, rank // n, LANES), F32),
            jax.ShapeDtypeStruct(start.shape, F32),
        ],
        scratch_shapes=[
            pltpu.VMEM((rank, rows), F32),
            pltpu.VMEM((left * depth, rows, width), F32),
            pltpu.VMEM((halves, left * depth, rank, LANES), F32),
            pltpu.VMEM((2, piece, rows, width), F32),
            pltpu.VMEM((halves, size, rank // n, LANES), F32),
            pltpu.VMEM((size, size), F32),
            pltpu.VMEM((size, size), F32),
            dma((left, n - 1)),
            dma((left, n - 1)),
            dma((left,)),
            dma((left,)),
            dma((2,)),
            dma,
        ]
        + sum_scratch(size, nx, n),
        compiler_params=pltpu.CompilerParams(
            collective_id=1, has_side_effects=True, vmem_limit_bytes=VMEM_LIMIT
        ),
    )(unfolded, factor, start)


def core_kernel(halves, *refs):
    *x_refs, f_ref, o_ref = refs
    factor = split(f_ref[...].T)
    rows = f_ref.shape[0]
    for r in range(8):
        parts = [
            ref.at[0].reshape(rows * 8, LANES)[pl.ds(r, rows, stride=8), :] for ref in x_refs
        ]
        values = parts[0] if halves == 1 else jnp.concatenate(parts, axis=1)
        o_ref[r] = product(factor, split(values), NN).T


def core(reduced, factor):
    halves, rows, ranks, _ = reduced.shape
    width = halves * LANES
    kept = factor.shape[1]
    specs = [
        pl.BlockSpec((1, rows, 8, LANES), functools.partial(lambda h, r: (h, 0, r, 0), h))
        for h in range(halves)
    ]
    return pl.pallas_call(
        functools.partial(core_kernel, halves),
        grid=(ranks // 8,),
        in_specs=specs + [pl.BlockSpec((rows, kept), lambda r: (0, 0))],
        out_specs=pl.BlockSpec((8, width, kept), lambda r: (r, 0, 0)),
        out_shape=jax.ShapeDtypeStruct((ranks, width, kept), F32),
        compiler_params=pltpu.CompilerParams(vmem_limit_bytes=VMEM_LIMIT),
    )(*[reduced] * halves, factor)


def lower_inverse(products):
    size = products.shape[0]
    group = 8
    count = size // 8
    tiles = [products[8 * t : 8 * t + 8, :] for t in range(count)]
    pivots = [None] * count
    lane = lax.broadcasted_iota(jnp.int32, (8, size), 1)
    row = lax.broadcasted_iota(jnp.int32, (8, size), 0)

    def across(tile, k):
        return jnp.broadcast_to(tile[:, k : k + 1], tile.shape)

    def down(tile, r):
        return jnp.broadcast_to(tile[r : r + 1, :], tile.shape)

    for k in range(0, size, group):
        first = k // 8
        columns = [[across(tiles[t], k + s) for t in range(first, count)] for s in range(group)]
        inside = (lane >= k) & (lane < k + group)
        for t in range(first, count):
            eye = jnp.where(lane == row + 8 * t, 1.0, 0.0)
            tiles[t] = jnp.where(inside, eye, tiles[t])
        for s in range(group):
            r = k + s - 8 * first
            pivot = down(columns[s][0], r)
            pivots[first] = (
                pivot if pivots[first] is None else jnp.where(row >= r, pivot, pivots[first])
            )
            inverse = 1.0 / pivot
            factors = [column * inverse for column in columns[s]]
            factors[0] = jnp.where(row > r, factors[0], 0.0)
            for later in range(s + 1, group):
                head = down(columns[later][0], r)
                columns[later] = [c - f * head for c, f in zip(columns[later], factors)]
            head = down(tiles[first], r)
            for t in range(first, count):
                tiles[t] = tiles[t] - factors[t - first] * head
    rows = [
        jnp.where(lane <= row + 8 * t, tiles[t] * lax.rsqrt(pivots[t]), 0.0) for t in range(count)
    ]
    return jnp.concatenate(rows, axis=0)


def subspace_steps(g_ref, q_ref, o_ref):
    dot = functools.partial(
        lax.dot_general, precision=lax.Precision.HIGHEST, preferred_element_type=F32
    )
    source = q_ref
    for sweep in range(SWEEPS):
        projected = dot(g_ref[...], source[...], NN)
        inverse = lower_inverse(dot(projected, projected, TN))
        o_ref[...] = dot(projected, inverse, NT)
        source = o_ref


def shards(nx, ny, state_field, start_one, start_two):
    snapshots, variables, cells = state_field.shape[2:]
    rank = start_one.shape[1]
    chunks, passed, window = 16, 12, 4
    unfolded, factor_one = gather(state_field, start_one, nx, ny, chunks, passed, window)
    reduced, factor_two = reduce_exchange(unfolded, factor_one, start_two, nx, chunks, passed)
    packed = core(reduced, factor_two)
    packed = packed.reshape(rank // ny, snapshots, variables, cells // nx, rank)
    return packed.transpose(0, 4, 1, 2, 3), factor_one, factor_two


def solution(mesh):
    placed = (P("gx", "gy", None, None, None), P(), P())
    return jax.shard_map(
        functools.partial(shards, mesh.shape["gx"], mesh.shape["gy"]),
        mesh=mesh,
        in_specs=placed,
        out_specs=(P("gy", None, None, None, "gx"), P(), P()),
        check_vma=False,
    )
```
